512 devices in a mesh: group: 16 (over y, z_lo), fsdp: 32 (over z_hi, x, core).
Axes of the slice: x: 4, y: 8, z: 8 (z_hi: 4, z_lo: 2; z = z_hi * 2 + z_lo), core: 2. Of those that a mesh axis runs over, the one named last changes fastest.
Arguments:
- activations: bfloat16 [16, 5120, 5120], P('group', 'fsdp'), may hold values from -6 to 6
- cotangent: bfloat16 [16, 5120, 1024], P('group', 'fsdp'), may hold values from -384 to 384
- live: int32 [16, 32], P('group', 'fsdp'), may hold values from 1 to 160, as said below
- local_params: bfloat16 [16, 5120, 1024], P('group', 'fsdp'), may hold values from -6 to 6
- anchor: float32 [32, 160, 1024], P('fsdp', 'group'), may hold values from -6 to 6
- momentum: float32 [32, 160, 1024], P('fsdp', 'group'), may hold values from -6 to 6
Outputs:
- new_params: bfloat16 [5120, 1024], P('fsdp')
- new_anchor: float32 [32, 160, 1024], P('fsdp', 'group')
- new_momentum: float32 [32, 160, 1024], P('fsdp', 'group')
The draws below stay inside these ranges and needn't reach their ends.
Inputs may be any that keep to these rules, and one draw needn't show every extreme that they name: Within a group the live counts of its devices are independent; one device of the last group is full.
All inputs are finite; a program needn't handle non-finite values.
Results may differ from the reference program's by a relative error of at most 0.0095.
Values may be sent and summed in bfloat16 or wider, within the bound.
A program may use at most 64 MiB of HBM per device.

```python
import jax
import jax.numpy as jnp
from jax import lax

D = 5120
TOK_DEV = 160
COLS = 1024
GROUPS = 16
FSDP_BLOCKS = 32
ROWS_DEV = 160
GROUP_TOK = 5120


def draw_live(key, part):
    key = jax.random.fold_in(key, 11)
    rank = jnp.arange(GROUPS, dtype=jnp.int32)[:, None]
    low = TOK_DEV // 8 + 5 * TOK_DEV // 8 * rank // max(GROUPS - 1, 1)
    extra = jax.random.randint(key, (GROUPS, FSDP_BLOCKS), 0, TOK_DEV // 4 + 1)
    counts = jnp.clip(low + extra, 1, TOK_DEV)
    counts = counts.at[GROUPS - 1, 0].set(TOK_DEV)
    return counts.astype(jnp.int32)


def block_scale(rng, shape, split, smallest, top_value):
    factor_of = 1.0
    for dim, parts in split:
        steps = jax.random.uniform(jax.random.fold_in(jax.random.fold_in(rng, 6), dim), (parts,), jnp.float32, smallest / len(split), top_value / len(split))
        factor_of = factor_of * jnp.repeat(jnp.exp(steps), shape[dim] // parts).reshape((-1,) + (1,) * (len(shape) - 1 - dim))
    return factor_of


def centred(stream_key, dims, deviation, bound, shards=(), kind=jnp.bfloat16):
    values = deviation * jax.random.normal(stream_key, dims, jnp.float32)
    if shards:
        values = values * block_scale(stream_key, dims, shards, -0.22, 0.18)
    return jnp.clip(values, -bound, bound).astype(kind)


def setup_inputs(seed: int = 0) -> dict:
    keys = jax.random.split(jax.random.key(seed), 7)
    activations = centred(keys[0], (GROUPS, GROUP_TOK, D), 1.0, 6.0, ((0, 16), (1, 32)))
    cotangent = centred(keys[1], (GROUPS, GROUP_TOK, COLS), 64.0, 384.0, ((0, 16), (1, 32)))
    live = draw_live(jax.random.fold_in(keys[6], 71), 0)
    local_params = centred(keys[3], (GROUPS, D, COLS), 1.0, 6.0, ((0, 16), (1, 32)))
    anchor = centred(keys[4], (FSDP_BLOCKS, ROWS_DEV, COLS), 1.0, 6.0, ((0, 32), (1, 16)), jnp.float32)
    momentum = centred(keys[5], (FSDP_BLOCKS, ROWS_DEV, COLS), 1.0, 6.0, ((0, 32), (1, 16)), jnp.float32)
    return {"activations": activations, "cotangent": cotangent, "live": live, "local_params": local_params, "anchor": anchor, "momentum": momentum}


def reference(activations, cotangent, live, local_params, anchor, momentum):
    slots = jnp.arange(GROUP_TOK, dtype=jnp.int32)
    owner = slots // TOK_DEV
    within = slots % TOK_DEV
    count = jnp.sum(live, axis=1).astype(jnp.float32)
    total = jnp.sum(count)

    def one_group(carry, index):
        limit = live[index][owner]
        keep = within < limit
        masked = jnp.where(keep[:, None], cotangent[index], jnp.zeros_like(cotangent[index]))
        grad = jnp.dot(activations[index].T, masked, preferred_element_type=jnp.float32) / count[index]
        inner = local_params[index].astype(jnp.float32) - 0.5 * grad
        return carry + (count[index] / total) * inner, None

    average, unused = lax.scan(one_group, jnp.zeros((D, COLS), jnp.float32), jnp.arange(GROUPS, dtype=jnp.int32))
    whole = anchor.reshape(D, COLS)
    delta = whole - average
    moment = 0.9 * momentum.reshape(D, COLS) + delta
    updated = whole - 0.7 * (delta + 0.9 * moment)
    return updated.astype(jnp.bfloat16), updated.reshape(FSDP_BLOCKS, ROWS_DEV, COLS), moment.reshape(FSDP_BLOCKS, ROWS_DEV, COLS)
```

```python
import jax
import jax.numpy as jnp
from jax import lax
from jax.experimental import pallas as pl
from jax.experimental.pallas import tpu as pltpu
from jax.sharding import PartitionSpec as P

MESH = pl.DeviceIdType.MESH
BF, F32 = jnp.bfloat16, jnp.float32
SIZE = {"x": 4, "y": 8, "z": 8}
UNITS = ("xyz", "xzy", "yxz", "zxy", "zxy")
NU = len(UNITS)
TILE = (16, 128)
TOK, ROWS, COLS, LIN = 160, 160, 1024, 80
VMEM_LIMIT = 56_000_000


def coords():
    g, f = lax.axis_index("group"), lax.axis_index("fsdp")
    return {"x": (f // 2) % 4, "y": g // 2, "z": (f // 8) * 2 + g % 2, "c": f % 2}


def device(at):
    return (at["y"] * 2 + at["z"] % 2, (at["z"] // 2) * 8 + at["x"] * 2 + at["c"])


def peer(here, axis, step):
    n = SIZE[axis]
    return device({**here, axis: (here[axis] + step + n) % n})


def loop(n, body, start=0):
    def step(i, carry):
        body(i)
        return carry

    lax.fori_loop(start, n, step, 0)


def put(src, dst, ssem, rsem, to):
    return pltpu.make_async_remote_copy(
        src_ref=src, dst_ref=dst, send_sem=ssem, recv_sem=rsem, device_id=to, device_id_type=MESH
    )


class Ring:
    def __init__(self, here, sign, axis, part, far, near, fs, fr, ns, nr):
        self.here, self.sign, self.axis, self.part = here, sign, axis, part
        self.n, self.me = SIZE[axis], here[axis]
        self.far, self.near = far, near
        self.sems = (fs, fr, ns, nr)

    def _far(self, k):
        t = (self.me + self.sign * (self.n // 2 - k) + self.n) % self.n
        to = peer(self.here, self.axis, self.sign)
        return t, put(self.part.at[t], self.far.at[k], self.sems[0].at[k], self.sems[1].at[k], to)

    def _near(self, k):
        t = (self.me - self.sign * (self.n // 2 - 1 - k) + self.n) % self.n
        to = peer(self.here, self.axis, -self.sign)
        return t, put(self.part.at[t], self.near.at[k], self.sems[2].at[k], self.sems[3].at[k], to)

    def _add(self, t, got):
        def body(i):
            self.part[t, i] = (self.part[t, i].astype(F32) + got[i].astype(F32)).astype(BF)

        loop(self.part.shape[1], body)

    def send_far(self, k):
        t, copy = self._far(k)
        if k:
            self._far(k - 1)[1].wait_recv()
            self._add(t, self.far.at[k - 1])
        copy.start()

    def send_near(self, k):
        t, copy = self._near(k)
        if k:
            self._near(k - 1)[1].wait_recv()
            self._add(t, self.near.at[k - 1])
        copy.start()

    def finish(self):
        h = self.n // 2
        self._far(h - 1)[1].wait_recv()
        self._near(h - 2)[1].wait_recv()
        a, b = self.far.at[h - 1], self.near.at[h - 2]

        def body(i):
            total = self.part[self.me, i].astype(F32) + a[i].astype(F32) + b[i].astype(F32)
            self.part[self.me, i] = total.astype(BF)

        loop(self.part.shape[1], body)
        return self.part.at[self.me]

    def drain(self):
        for k in range(self.n // 2):
            self._far(k)[1].wait_send()
        for k in range(self.n // 2 - 1):
            self._near(k)[1].wait_send()


class Direct:
    def __init__(self, here, axis, part, slots, ss, rs):
        self.here, self.axis, self.part, self.slots = here, axis, part, slots
        self.n, self.me, self.ss, self.rs = SIZE[axis], here[axis], ss, rs

    def _copy(self, d):
        t = (self.me + d) % self.n
        to = peer(self.here, self.axis, d)
        return put(self.part.at[t], self.slots.at[d - 1], self.ss.at[d - 1], self.rs.at[d - 1], to)

    def start(self):
        loop(self.n, lambda d: self._copy(d).start(), 1)

    def arrive(self):
        loop(self.n, lambda d: self._copy(d).wait_recv(), 1)

    def total(self, i=None):
        at = (self.me,) if i is None else (self.me, i)
        acc = self.part[at].astype(F32)
        for d in range(self.n - 1):
            acc += self.slots[(d,) + at[1:]].astype(F32)
        return acc

    def drain(self):
        loop(self.n, lambda d: self._copy(d).wait_send(), 1)


def scratch():
    s = {}
    dma = pltpu.SemaphoreType.DMA
    s["a"], s["m"], s["lp"] = (pltpu.VMEM(v, BF) for v in ((TOK, 5120), (TOK, COLS), (ROWS, COLS)))
    s["anc"], s["mom"] = pltpu.VMEM((LIN, 128), F32), pltpu.VMEM((LIN, 128), F32)
    s["insem"] = dma((5,))
    s["at"] = pltpu.VMEM((2, 16, ROWS, TOK), BF)
    s["atp"] = pltpu.VMEM((16, ROWS, TOK), BF)
    s["mp"] = pltpu.VMEM((TOK, COLS), BF)
    s["exs"], s["exr"] = dma((3,)), dma((3,))
    s["cv"] = pltpu.VMEM((4, 8, 128), F32)
    s["cc"], s["cx"] = pltpu.VMEM((8, 128), F32), pltpu.VMEM((3, 8, 128), F32)
    s["cz"], s["cy"] = pltpu.VMEM((7, 8, 128), F32), pltpu.VMEM((7, 8, 128), F32)
    for k, n in (("cx", 3), ("cz", 7), ("cy", 7)):
        s[k + "s"], s[k + "r"] = dma((n,)), dma((n,))
    for u, order in enumerate(UNITS):
        n1, n2, n3 = (SIZE[k] for k in order)
        s[f"u{u}"] = pltpu.VMEM((n1, n2, n3) + TILE, BF)
        s[f"far{u}"] = pltpu.VMEM((n1 // 2, n2, n3) + TILE, BF)
        s[f"near{u}"] = pltpu.VMEM((n1 // 2 - 1, n2, n3) + TILE, BF)
        s[f"fs{u}"], s[f"fr{u}"] = dma((n1 // 2,)), dma((n1 // 2,))
        s[f"ns{u}"], s[f"nr{u}"] = dma((n1 // 2 - 1,)), dma((n1 // 2 - 1,))
        s[f"two{u}"] = pltpu.VMEM((n2 - 1, n3) + TILE, BF)
        s[f"ts{u}"], s[f"tr{u}"] = dma((n2 - 1,)), dma((n2 - 1,))
        s[f"v{u}"] = pltpu.VMEM((n3,) + TILE, BF)
        s[f"three{u}"] = pltpu.VMEM((n3 - 1,) + TILE, BF)
        s[f"hs{u}"], s[f"hr{u}"] = dma((n3 - 1,)), dma((n3 - 1,))
    s["base"] = pltpu.VMEM((16, LIN, 128), BF)
    s["basef"] = pltpu.VMEM((ROWS * 8, 128), F32)
    s["bs"], s["br"] = dma((15,)), dma((15,))
    s["ag"] = pltpu.VMEM((16, NU) + TILE, BF)
    s["as"], s["ar"] = dma((15,)), dma((15,))
    s["avg"] = pltpu.VMEM((ROWS * 8, 128), F32)
    return s


NAMES = tuple(scratch())


def kernel(live_ref, a_hbm, m_hbm, lp_hbm, anc_hbm, mom_hbm, np_ref, na_ref, nm_ref, *refs):
    s = dict(zip(NAMES, refs))
    anc_ref, mom_ref = s["anc"], s["mom"]
    here = coords()
    x, y, z, c = (here[k] for k in "xyzc")
    zl, g = z % 2, y * 2 + z % 2
    sign = 1 - 2 * c
    partner = device({**here, "c": 1 - c})

    def group_peer(j):
        other = (g + j) % 16
        return (other, lax.axis_index("fsdp"))

    bar = pltpu.get_barrier_semaphore()

    def greet(to):
        pl.semaphore_signal(bar, inc=1, device_id=to, device_id_type=MESH)

    greet(partner)
    loop(4, lambda d: greet(peer(here, "x", d)), 1)
    loop(8, lambda d: greet(peer(here, "z", d)), 1)
    loop(16, lambda j: greet(group_peer(j)), 1)

    wanted = ((a_hbm, s["a"]), (m_hbm, s["m"]), (lp_hbm, s["lp"]), (anc_hbm, anc_ref), (mom_hbm, mom_ref))
    loads = [pltpu.make_async_copy(src, dst, s["insem"].at[i]) for i, (src, dst) in enumerate(wanted)]
    for load in loads:
        load.start()

    live = live_ref[0, 0]
    s["cv"][0] = jnp.full((8, 128), live.astype(F32), F32)

    loads[1].wait()
    row = lax.broadcasted_iota(jnp.int32, (TOK, COLS), 0)
    s["m"][...] = jnp.where(row < live, s["m"][...].astype(F32), 0.0).astype(BF)
    loads[0].wait()

    def transpose(k):
        t = s["a"][:, pl.ds(pl.multiple_of(k * 640, 128), 640)].T
        for j in range(4):
            s["at"][j % 2, 2 * k + j // 2] = t[j * 160:(j + 1) * 160]

    loop(8, transpose)
    for load in loads[2:]:
        load.wait()
    s["base"][g] = (-0.33 * anc_ref[...] - 0.567 * mom_ref[...]).astype(BF)

    pl.semaphore_wait(bar, 1 + 3 + 7 + 15)

    ex = [put(s["cv"].at[0], s["cc"], s["exs"].at[2], s["exr"].at[2], partner),
          put(s["m"], s["mp"], s["exs"].at[1], s["exr"].at[1], partner),
          put(s["at"].at[1 - c], s["atp"], s["exs"].at[0], s["exr"].at[0], partner)]
    for copy in ex:
        copy.start()

    def base_copy(j):
        return put(s["base"].at[g], s["base"].at[g], s["bs"].at[j - 1], s["br"].at[j - 1], group_peer(j))

    def base_in(j):
        src = (g - j + 16) % 16
        return put(s["base"].at[src], s["base"].at[src], s["bs"].at[j - 1], s["br"].at[j - 1], group_peer(j))

    def count_copy(key, axis, d, k):
        return put(s["cv"].at[k], s[key].at[d - 1], s[key + "s"].at[d - 1], s[key + "r"].at[d - 1], peer(here, axis, d))

    ex[0].wait_recv()
    s["cv"][1] = s["cv"][0] + s["cc"][...]
    loop(4, lambda d: count_copy("cx", "x", d, 1).start(), 1)
    loop(16, lambda j: base_copy(j).start(), 1)

    rings, twos, threes = [], [], []
    for u, order in enumerate(UNITS):
        rings.append(Ring(here, sign, order[0], s[f"u{u}"], s[f"far{u}"], s[f"near{u}"],
                          s[f"fs{u}"], s[f"fr{u}"], s[f"ns{u}"], s[f"nr{u}"]))

    ex[1].wait_recv()
    ex[2].wait_recv()

    def block(dz, dx, own=None):
        bz, bx = (z // 2 + dz) % 4, (x + dx) % 4
        blk = bz * 4 + bx
        for h in range(2):
            cols = slice(h * 512, (h + 1) * 512)
            acc = jnp.dot(s["at"][c, blk], s["m"][:, cols], preferred_element_type=F32)
            acc += jnp.dot(s["atp"][blk], s["mp"][:, cols], preferred_element_type=F32)
            if own is not None:
                acc -= (2.0 * own) * s["lp"][:, cols].astype(F32)
            out = acc.astype(BF)
            for u, order in enumerate(UNITS):
                for q in range(2):
                    for t in range(4):
                        at = {"x": bx, "y": h * 4 + t, "z": bz * 2 + q}
                        s[f"u{u}"][at[order[0]], at[order[1]], at[order[2]]] = (
                            out[u * 32 + q * 16:u * 32 + q * 16 + 16, t * 128:(t + 1) * 128])

    loop(4, lambda i: block(2, i))
    for u in (3, 4):
        rings[u].send_far(0)

    loop(4, lambda d: count_copy("cx", "x", d, 1).wait_recv(), 1)
    s["cv"][2] = s["cv"][1] + s["cx"][0] + s["cx"][1] + s["cx"][2]
    loop(8, lambda d: count_copy("cz", "z", d, 2).start(), 1)

    loop(3, lambda i: block((i + 3) % 4, 2))
    for u in (0, 1):
        rings[u].send_far(0)
    loop(8, lambda i: block(jnp.maximum(3 - 2 * (i // 3), 0), jnp.maximum(3 - 2 * (i % 3), 0)))
    for u in (0, 1):
        rings[u].send_near(0)

    loop(8, lambda d: count_copy("cz", "z", d, 2).wait_recv(), 1)
    cz = s["cz"]
    count = s["cv"][2] + cz[1] + cz[3] + cz[5]
    s["cv"][3] = count + cz[0] + cz[2] + cz[4] + cz[6]
    loop(8, lambda d: count_copy("cy", "y", d, 3).start(), 1)
    block(0, 0, count[0:1, 0:1])
    rings[2].send_far(0)
    for u in (2, 3, 4):
        rings[u].send_near(0)

    def second(u):
        part = rings[u].finish()
        d = Direct(here, UNITS[u][1], part, s[f"two{u}"], s[f"ts{u}"], s[f"tr{u}"])
        d.start()
        twos.append(d)
        return d

    def third(u, d):
        d.arrive()

        def body(i):
            s[f"v{u}"][i] = d.total(i).astype(BF)

        loop(SIZE[UNITS[u][2]], body)
        e = Direct(here, UNITS[u][2], s[f"v{u}"], s[f"three{u}"], s[f"hs{u}"], s[f"hr{u}"])
        e.start()
        threes.append(e)
        return e

    rings[2].send_far(1)
    for u in (3, 4):
        rings[u].send_far(1)
    rings[2].send_near(1)
    for u in (3, 4):
        rings[u].send_near(1)
    rings[2].send_far(2)
    rings[2].send_near(2)
    for u in (0, 1):
        rings[u].send_far(1)
    rings[2].send_far(3)
    for u in (3, 4):
        rings[u].send_far(2)
        rings[u].send_near(2)
    d2 = second(2)
    loop(8, lambda d: count_copy("cy", "y", d, 3).wait_recv(), 1)
    total = s["cv"][3]
    for k in range(7):
        total += s["cy"][k]
    loop(16, lambda j: base_in(j).wait_recv(), 1)

    def widen(j):
        s["basef"][pl.ds(pl.multiple_of(j * LIN, 8), LIN), :] = s["base"][j].astype(F32)

    loop(16, widen)
    scale = (-0.5 / total)[0:1, 0:1]

    for u in (3, 4):
        rings[u].send_far(3)
    d0, d1 = second(0), second(1)
    e2 = third(2, d2)
    d3, d4 = second(3), second(4)
    e0, e1 = third(0, d0), third(1, d1)
    e3, e4 = third(3, d3), third(4, d4)

    for u, e in ((2, e2), (0, e0), (1, e1), (3, e3), (4, e4)):
        e.arrive()
        s["ag"][g, u] = (scale * e.total()).astype(BF)

    def ag_copy(j):
        return put(s["ag"].at[g], s["ag"].at[g], s["as"].at[j - 1], s["ar"].at[j - 1], group_peer(j))

    def ag_in(j):
        src = (g - j + 16) % 16
        return put(s["ag"].at[src], s["ag"].at[src], s["as"].at[j - 1], s["ar"].at[j - 1], group_peer(j))

    loop(16, lambda j: ag_copy(j).start(), 1)

    for r in rings:
        r.drain()
    for d in twos + threes:
        d.drain()
    for copy in ex:
        copy.wait_send()
    for key, axis, k, n in (("cx", "x", 1, 4), ("cz", "z", 2, 8), ("cy", "y", 3, 8)):
        loop(n, lambda d, key=key, axis=axis, k=k: count_copy(key, axis, d, k).wait_send(), 1)
    loop(16, lambda j: base_copy(j).wait_send(), 1)

    loop(16, lambda j: ag_in(j).wait_recv(), 1)
    for yy in range(8):
        for q in range(2):
            for u in range(NU):
                r0 = u * 32 + q * 16
                avg = s["ag"][yy * 2 + q, u].astype(F32)
                s["avg"][pl.ds(r0 * 8 + yy, 16, stride=8), :] = avg
                base = s["basef"][pl.ds(r0 * 8 + yy, 16, stride=8), :]
                np_ref[r0:r0 + 16, yy * 128:(yy + 1) * 128] = (base + 1.33 * avg).astype(BF)
    own = s["avg"][pl.ds(pl.multiple_of(g * LIN, 8), LIN), :]
    anc = anc_ref[...]
    delta = anc - own
    moment = 0.9 * mom_ref[...] + delta
    nm_ref[...] = moment
    na_ref[...] = anc - 0.7 * (delta + 0.9 * moment)
    loop(16, lambda j: ag_copy(j).wait_send(), 1)


def local(activations, cotangent, live, local_params, anchor, momentum):
    vmem = pl.BlockSpec(memory_space=pltpu.VMEM)
    hbm = pl.BlockSpec(memory_space=pltpu.HBM)
    new_params, new_anchor, new_momentum = pl.pallas_call(
        kernel,
        name="outer_step",
        out_shape=(
            jax.ShapeDtypeStruct((ROWS, COLS), BF),
            jax.ShapeDtypeStruct((LIN, 128), F32),
            jax.ShapeDtypeStruct((LIN, 128), F32),
        ),
        in_specs=[pl.BlockSpec(memory_space=pltpu.SMEM), hbm, hbm, hbm, hbm, hbm],
        out_specs=(vmem, vmem, vmem),
        scratch_shapes=list(scratch().values()),
        compiler_params=pltpu.CompilerParams(
            collective_id=0, has_side_effects=True, vmem_limit_bytes=VMEM_LIMIT
        ),
    )(live, activations[0], cotangent[0], local_params[0], anchor.reshape(LIN, 128), momentum.reshape(LIN, 128))
    return new_params, new_anchor.reshape(1, 10, COLS), new_momentum.reshape(1, 10, COLS)


def solution(mesh):
    in_specs = (
        P("group", "fsdp", None),
        P("group", "fsdp", None),
        P("group", "fsdp"),
        P("group", "fsdp", None),
        P("fsdp", "group", None),
        P("fsdp", "group", None),
    )
    out_specs = (P("fsdp", None), P("fsdp", "group", None), P("fsdp", "group", None))
    return jax.shard_map(local, mesh=mesh, in_specs=in_specs, out_specs=out_specs, check_vma=False)
```

```python
import jax
import jax.numpy as jnp
from jax import lax
from jax.experimental import pallas as pl
from jax.experimental.pallas import tpu as pltpu
from jax.sharding import PartitionSpec as P

MESH = pl.DeviceIdType.MESH
BF, F32 = jnp.bfloat16, jnp.float32
SIZE = {"x": 4, "y": 8, "z": 8, "p": 8, "q": 8}
UNITS = ("xqp", "xpq", "yxz", "zxy", "pxq")
HALVES = 1
WAVES = ((0, 1, 2, 3, 4),)
PLAN = ("m0", "f00", "f10", "x", "m1", "n00", "n10", "m2", "m3", "f30", "n30", "t", "o", "f20", "n20", "f40", "n40",
        "q0", "f31", "n31", "f21", "n21", "f41", "n41", "f01", "q1", "f32", "n32", "f22", "n22", "f42", "n42",
        "f11", "s0", "q2", "c", "f33", "f23", "f43", "q3", "s1", "s2", "s3", "s4", "b",
        "h0", "h1", "h2", "h3", "h4", "w0", "d", "e0")
NU = len(UNITS)
TILE = (16, 128)
TOK, ROWS, COLS, LIN = 160, 160, 1024, 80
VMEM_LIMIT = 56_000_000


def coords():
    g, f = lax.axis_index("group"), lax.axis_index("fsdp")
    return with_pq({"x": (f // 2) % 4, "y": g // 2, "z": (f // 8) * 2 + g % 2, "c": f % 2})


def with_pq(at):
    c, y, z = at["c"], at["y"], at["z"]
    return {**at, "p": z + c * (y - z), "q": y + c * (z - y)}


def device(at):
    return (at["y"] * 2 + at["z"] % 2, (at["z"] // 2) * 8 + at["x"] * 2 + at["c"])


def peer(here, axis, step):
    n, c = SIZE[axis], here["c"]
    if axis in "pq":
        dy = step * (c if axis == "p" else 1 - c)
        return device({**here, "y": (here["y"] + dy + 8) % 8, "z": (here["z"] + step - dy + 8) % 8})
    return device({**here, axis: (here[axis] + step + n) % n})


def loop(n, body, start=0):
    def step(i, carry):
        body(i)
        return carry

    lax.fori_loop(start, n, step, 0)


def put(src, dst, ssem, rsem, to):
    return pltpu.make_async_remote_copy(
        src_ref=src, dst_ref=dst, send_sem=ssem, recv_sem=rsem, device_id=to, device_id_type=MESH
    )


class Ring:
    def __init__(self, here, sign, axis, part, far, near, fs, fr, ns, nr):
        self.here, self.sign, self.axis, self.part = here, sign, axis, part
        self.n, self.me = SIZE[axis], here[axis]
        self.far, self.near = far, near
        self.sems = (fs, fr, ns, nr)
        self.width = part.shape[1] // HALVES

    def _cut(self, h):
        return slice(h * self.width, (h + 1) * self.width)

    def _far(self, k, h):
        t = (self.me + self.sign * (self.n // 2 - k) + self.n) % self.n
        to = peer(self.here, self.axis, self.sign)
        src, dst = self.part.at[t, self._cut(h)], self.far.at[k, self._cut(h)]
        return t, put(src, dst, self.sems[0].at[k, h], self.sems[1].at[k, h], to)

    def _near(self, k, h):
        t = (self.me - self.sign * (self.n // 2 - 1 - k) + self.n) % self.n
        to = peer(self.here, self.axis, -self.sign)
        src, dst = self.part.at[t, self._cut(h)], self.near.at[k, self._cut(h)]
        return t, put(src, dst, self.sems[2].at[k, h], self.sems[3].at[k, h], to)

    def _add(self, t, got, h):
        cut = self._cut(h)
        self.part[t, cut] = self.part[t, cut] + got[cut]

    def send_far(self, k, h):
        t, copy = self._far(k, h)
        if k:
            self._far(k - 1, h)[1].wait_recv()
            self._add(t, self.far.at[k - 1], h)
        copy.start()

    def send_near(self, k, h):
        t, copy = self._near(k, h)
        if k:
            self._near(k - 1, h)[1].wait_recv()
            self._add(t, self.near.at[k - 1], h)
        copy.start()

    def finish(self):
        n = self.n // 2
        a, b = self.far.at[n - 1], self.near.at[n - 2]

        def body(i):
            total = self.part[self.me, i].astype(F32) + a[i].astype(F32) + b[i].astype(F32)
            self.part[self.me, i] = total.astype(BF)

        for h in range(HALVES):
            self._near(n - 2, h)[1].wait_recv()
            self._far(n - 1, h)[1].wait_recv()
            loop((h + 1) * self.width, body, h * self.width)
        return self.part.at[self.me]

    def drain(self):
        for h in range(HALVES):
            for k in range(self.n // 2):
                self._far(k, h)[1].wait_send()
            for k in range(self.n // 2 - 1):
                self._near(k, h)[1].wait_send()


class Direct:
    def __init__(self, here, axis, part, slots, ss, rs):
        self.here, self.axis, self.part, self.slots = here, axis, part, slots
        self.n, self.me, self.ss, self.rs = SIZE[axis], here[axis], ss, rs

    def _copy(self, d):
        t = (self.me + d) % self.n
        to = peer(self.here, self.axis, d)
        return put(self.part.at[t], self.slots.at[d - 1], self.ss.at[d - 1], self.rs.at[d - 1], to)

    def start(self):
        loop(self.n, lambda d: self._copy(d).start(), 1)

    def arrive(self):
        loop(self.n, lambda d: self._copy(d).wait_recv(), 1)

    def total(self, i=None):
        at = (self.me,) if i is None else (self.me, i)
        acc = self.part[at].astype(F32)
        for d in range(self.n - 1):
            acc += self.slots[(d,) + at[1:]].astype(F32)
        return acc

    def drain(self):
        loop(self.n, lambda d: self._copy(d).wait_send(), 1)


def scratch():
    s = {}
    dma = pltpu.SemaphoreType.DMA
    s["a"], s["m"], s["lp"] = (pltpu.VMEM(v, BF) for v in ((TOK, 5120), (TOK, COLS), (ROWS, COLS)))
    s["anc"], s["mom"] = pltpu.VMEM((LIN, 128), F32), pltpu.VMEM((LIN, 128), F32)
    s["insem"] = dma((6,))
    s["at"] = pltpu.VMEM((2, 4, 4 * ROWS, TOK), BF)
    s["atp"] = pltpu.VMEM((4, 4 * ROWS, TOK), BF)
    s["live"] = pltpu.VMEM((1, 1), jnp.int32)
    s["mp"] = pltpu.VMEM((TOK, COLS), BF)
    s["exs"], s["exr"] = dma((6,)), dma((6,))
    s["cv"] = pltpu.VMEM((4, 8, 128), F32)
    s["cc"], s["cx"] = pltpu.VMEM((8, 128), F32), pltpu.VMEM((3, 8, 128), F32)
    s["cz"], s["cy"] = pltpu.VMEM((7, 8, 128), F32), pltpu.VMEM((7, 8, 128), F32)
    for k, n in (("cx", 3), ("cz", 7), ("cy", 7)):
        s[k + "s"], s[k + "r"] = dma((n,)), dma((n,))
    for u, order in enumerate(UNITS):
        n1, n2, n3 = (SIZE[k] for k in order)
        s[f"u{u}"] = pltpu.VMEM((n1, n2, n3) + TILE, BF)
        s[f"far{u}"] = pltpu.VMEM((n1 // 2, n2, n3) + TILE, BF)
        s[f"near{u}"] = pltpu.VMEM((n1 // 2 - 1, n2, n3) + TILE, BF)
        s[f"fs{u}"], s[f"fr{u}"] = dma((n1 // 2, HALVES)), dma((n1 // 2, HALVES))
        s[f"ns{u}"], s[f"nr{u}"] = dma((n1 // 2 - 1, HALVES)), dma((n1 // 2 - 1, HALVES))
        s[f"two{u}"] = pltpu.VMEM((n2 - 1, n3) + TILE, BF)
        s[f"ts{u}"], s[f"tr{u}"] = dma((n2 - 1,)), dma((n2 - 1,))
        s[f"v{u}"] = pltpu.VMEM((n3,) + TILE, BF)
        s[f"three{u}"] = pltpu.VMEM((n3 - 1,) + TILE, BF)
        s[f"hs{u}"], s[f"hr{u}"] = dma((n3 - 1,)), dma((n3 - 1,))
    s["base"] = pltpu.VMEM((16, LIN, 128), BF)
    s["basef"] = pltpu.VMEM((ROWS * 8, 128), F32)
    s["bs"], s["br"] = dma((8,)), dma((8,))
    for w, units in enumerate(WAVES):
        s[f"ag{w}"] = pltpu.VMEM((16, len(units)) + TILE, BF)
        s[f"as{w}"], s[f"ar{w}"] = dma((15,)), dma((15,))
    s["avg"] = pltpu.VMEM((ROWS * 8, 128), F32)
    return s


NAMES = tuple(scratch())


def kernel(live_hbm, a_hbm, m_hbm, lp_hbm, anc_hbm, mom_hbm, np_ref, na_ref, nm_ref, *refs):
    s = dict(zip(NAMES, refs))
    anc_ref, mom_ref = s["anc"], s["mom"]
    here = coords()
    x, y, z, c = (here[k] for k in "xyzc")
    zl, g = z % 2, y * 2 + z % 2
    sign = 1 - 2 * c
    partner = device({**here, "c": 1 - c})

    def group_peer(j):
        other = (g + j) % 16
        return (other, lax.axis_index("fsdp"))

    bar = pltpu.get_barrier_semaphore()

    def greet(to):
        pl.semaphore_signal(bar, inc=1, device_id=to, device_id_type=MESH)

    greet(partner)
    loop(4, lambda d: greet(peer(here, "x", d)), 1)
    loop(8, lambda d: greet(peer(here, "z", d)), 1)
    loop(16, lambda j: greet(group_peer(j)), 1)

    wanted = ((live_hbm, s["live"]), (m_hbm, s["m"]), (a_hbm, s["a"]),
              (lp_hbm, s["lp"]), (anc_hbm, anc_ref), (mom_hbm, mom_ref))
    loads = [pltpu.make_async_copy(src, dst, s["insem"].at[i]) for i, (src, dst) in enumerate(wanted)]
    for load in loads:
        load.start()

    loads[0].wait()
    live = s["live"][...]
    s["cv"][0] = jnp.broadcast_to(live.astype(F32), (8, 128))
    loads[1].wait()
    row = lax.broadcasted_iota(jnp.int32, (TOK, COLS), 0)
    s["m"][...] = jnp.where(row < live, s["m"][...].astype(F32), 0.0).astype(BF)
    loads[2].wait()

    def transpose(k):
        t = s["a"][:, pl.ds(pl.multiple_of(k * 640, 128), 640)].T
        for j in range(4):
            at = pl.multiple_of((k % 2) * 320 + (j // 2) * 160, 16)
            s["at"][j % 2, k // 2, pl.ds(at, 160)] = t[j * 160:(j + 1) * 160]

    loop(8, transpose)
    for load in loads[3:]:
        load.wait()
    s["base"][g] = (-0.33 * anc_ref[...] - 0.567 * mom_ref[...]).astype(BF)

    pl.semaphore_wait(bar, 1 + 3 + 7 + 15)

    def rows_of(bx):
        return pl.ds(pl.multiple_of(bx * ROWS, 16), ROWS)

    def ex_copy(i, bx):
        rows = rows_of(bx)
        return put(s["at"].at[1 - c, :, rows], s["atp"].at[:, rows], s["exs"].at[2 + i], s["exr"].at[2 + i], partner)

    ex = [put(s["cv"].at[0], s["cc"], s["exs"].at[0], s["exr"].at[0], partner),
          put(s["m"], s["mp"], s["exs"].at[1], s["exr"].at[1], partner)]
    ex += [ex_copy(i, (x + dx + 4) % 4) for i, dx in enumerate((2, sign, -sign, 0))]
    for copy in ex[:4]:
        copy.start()

    zpartner = device({**here, "z": z + 1 - 2 * zl})
    base_z = put(s["base"].at[g], s["base"].at[g], s["bs"].at[7], s["br"].at[7], zpartner)

    def base_ring(k, way):
        pair = s["base"].at[pl.ds(2 * ((y - way * sign * k + 8) % 8), 2)]
        i = k if way > 0 else 4 + k
        return put(pair, pair, s["bs"].at[i], s["br"].at[i], peer(here, "y", way * sign))

    def base_step(k):
        if k == 0:
            base_z.wait_recv()
        else:
            base_ring(k - 1, 1).wait_recv()
            base_ring(k - 1, -1).wait_recv()
        base_ring(k, 1).start()
        if k < 3:
            base_ring(k, -1).start()

    def count_copy(key, axis, d, k):
        return put(s["cv"].at[k], s[key].at[d - 1], s[key + "s"].at[d - 1], s[key + "r"].at[d - 1], peer(here, axis, d))

    ex[0].wait_recv()
    s["cv"][1] = s["cv"][0] + s["cc"][...]
    loop(4, lambda d: count_copy("cx", "x", d, 1).start(), 1)
    base_z.start()

    rings = []
    for u, order in enumerate(UNITS):
        rings.append(Ring(here, sign, order[0], s[f"u{u}"], s[f"far{u}"], s[f"near{u}"],
                          s[f"fs{u}"], s[f"fr{u}"], s[f"ns{u}"], s[f"nr{u}"]))


    def store(out, bz, bx, r0, t0, width):
        for u, order in enumerate(UNITS):
            for q in range(2):
                for t in range(width):
                    at = with_pq({"x": bx, "y": t0 + t, "z": bz * 2 + q, "c": c})
                    r = r0 + u * 32 + q * 16
                    s[f"u{u}"][at[order[0]], at[order[1]], at[order[2]]] = out[r:r + 16, t * 128:(t + 1) * 128]

    def multiply(i):
        bx = (x + (2, -sign, sign, 0)[i] + 4) % 4
        rows = rows_of(bx)
        if i == 0:
            ex[1].wait_recv()
        ex_copy(i, bx).wait_recv()
        if i < 2:
            ex[4 + i].start()
        mine = s["at"][c, :, rows, :].reshape(4 * ROWS, TOK)
        theirs = s["atp"][:, rows, :].reshape(4 * ROWS, TOK)
        for h in range(4):
            cols = slice(h * 256, (h + 1) * 256)
            acc = jnp.dot(mine, s["m"][:, cols], preferred_element_type=F32)
            acc += jnp.dot(theirs, s["mp"][:, cols], preferred_element_type=F32)
            out = acc.astype(BF)
            for bz in range(4):
                store(out, bz, bx, bz * ROWS, h * 2, 2)

    def multiply_own(weight):
        rows = rows_of(x)
        for h in range(4):
            cols = slice(h * 256, (h + 1) * 256)
            acc = jnp.dot(s["at"][c, z // 2, rows], s["m"][:, cols], preferred_element_type=F32)
            acc += jnp.dot(s["atp"][z // 2, rows], s["mp"][:, cols], preferred_element_type=F32)
            acc -= weight * s["lp"][:, cols].astype(F32)
            store(acc.astype(BF), z // 2, x, 0, h * 2, 2)

    def far(u, k, h=None):
        for i in range(HALVES) if h is None else (h,):
            rings[u].send_far(k, i)

    def near(u, k, h=None):
        for i in range(HALVES) if h is None else (h,):
            rings[u].send_near(k, i)

    def second(u):
        part = rings[u].finish()
        d = Direct(here, UNITS[u][1], part, s[f"two{u}"], s[f"ts{u}"], s[f"tr{u}"])
        d.start()
        twos[u] = d

    def third(u):
        d = twos[u]
        d.arrive()

        def body(i):
            s[f"v{u}"][i] = d.total(i).astype(BF)

        loop(SIZE[UNITS[u][2]], body)
        e = Direct(here, UNITS[u][2], s[f"v{u}"], s[f"three{u}"], s[f"hs{u}"], s[f"hr{u}"])
        e.start()
        threes[u] = e

    def wave_send(w, total):
        for i, u in enumerate(WAVES[w]):
            threes[u].arrive()
            s[f"ag{w}"][g, i] = (total * threes[u].total()).astype(BF)
        for j in (8, 7, 9, 6, 10, 5, 11, 4, 12, 3, 13, 2, 14, 1, 15):
            ag_copy(w, j).start()

    def ag_copy(w, j):
        mine = s[f"ag{w}"].at[g]
        return put(mine, mine, s[f"as{w}"].at[j - 1], s[f"ar{w}"].at[j - 1], group_peer(j))

    def ag_in(w, j):
        theirs = s[f"ag{w}"].at[(g - j + 16) % 16]
        return put(theirs, theirs, s[f"as{w}"].at[j - 1], s[f"ar{w}"].at[j - 1], group_peer(j))

    def wave_end(w):
        loop(16, lambda j: ag_in(w, j).wait_recv(), 1)
        for i, u in enumerate(WAVES[w]):
            for yy in range(8):
                for q in range(2):
                    r0 = u * 32 + q * 16
                    avg = s[f"ag{w}"][yy * 2 + q, i].astype(F32)
                    s["avg"][pl.ds(r0 * 8 + yy, 16, stride=8), :] = avg
                    base = s["basef"][pl.ds(r0 * 8 + yy, 16, stride=8), :]
                    np_ref[r0:r0 + 16, yy * 128:(yy + 1) * 128] = (base + 1.33 * avg).astype(BF)

    twos, threes, known = {}, {}, {}

    def counts_x():
        loop(4, lambda d: count_copy("cx", "x", d, 1).wait_recv(), 1)
        s["cv"][2] = s["cv"][1] + s["cx"][0] + s["cx"][1] + s["cx"][2]
        loop(8, lambda d: count_copy("cz", "z", d, 2).start(), 1)

    def counts():
        loop(8, lambda d: count_copy("cz", "z", d, 2).wait_recv(), 1)
        cz = s["cz"]
        known["count"] = s["cv"][2] + cz[1] + cz[3] + cz[5]
        s["cv"][3] = known["count"] + cz[0] + cz[2] + cz[4] + cz[6]
        loop(8, lambda d: count_copy("cy", "y", d, 3).start(), 1)

    def total_count():
        loop(8, lambda d: count_copy("cy", "y", d, 3).wait_recv(), 1)
        total = s["cv"][3]
        for k in range(7):
            total += s["cy"][k]
        known["scale"] = (-0.5 / total)[0:1, 0:1]

    def base_rows():
        base_ring(3, 1).wait_recv()

        def widen(j):
            s["basef"][pl.ds(pl.multiple_of(j * LIN, 8), LIN), :] = s["base"][j].astype(F32)

        loop(16, widen)

    def drain():
        for r in rings:
            r.drain()
        for d in [*twos.values(), *threes.values()]:
            d.drain()
        for copy in ex:
            copy.wait_send()
        for key, axis, k, n in (("cx", "x", 1, 4), ("cz", "z", 2, 8), ("cy", "y", 3, 8)):
            loop(n, lambda d, key=key, axis=axis, k=k: count_copy(key, axis, d, k).wait_send(), 1)
        base_z.wait_send()
        for k in range(4):
            base_ring(k, 1).wait_send()
        for k in range(3):
            base_ring(k, -1).wait_send()

    steps = {
        "m": multiply, "q": base_step,
        "x": counts_x, "t": counts, "c": total_count, "b": base_rows, "d": drain,
        "o": lambda: multiply_own(2.0 * known["count"][0:1, 0:1]),
        "f": far, "n": near, "s": second, "h": third,
        "w": lambda w: wave_send(w, known["scale"]), "e": wave_end,
    }
    for step in PLAN:
        steps[step[0]](*(int(v) for v in step[1:]))

    own = s["avg"][pl.ds(pl.multiple_of(g * LIN, 8), LIN), :]
    anc = anc_ref[...]
    delta = anc - own
    moment = 0.9 * mom_ref[...] + delta
    nm_ref[...] = moment
    na_ref[...] = anc - 0.7 * (delta + 0.9 * moment)
    for w in range(len(WAVES)):
        loop(16, lambda j, w=w: ag_copy(w, j).wait_send(), 1)


def local(activations, cotangent, live, local_params, anchor, momentum):
    vmem = pl.BlockSpec(memory_space=pltpu.VMEM)
    hbm = pl.BlockSpec(memory_space=pltpu.HBM)
    new_params, new_anchor, new_momentum = pl.pallas_call(
        kernel,
        name="outer_step",
        out_shape=(
            jax.ShapeDtypeStruct((ROWS, COLS), BF),
            jax.ShapeDtypeStruct((LIN, 128), F32),
            jax.ShapeDtypeStruct((LIN, 128), F32),
        ),
        in_specs=[hbm] * 6,
        out_specs=(vmem, vmem, vmem),
        scratch_shapes=list(scratch().values()),
        compiler_params=pltpu.CompilerParams(
            collective_id=0, has_side_effects=True, vmem_limit_bytes=VMEM_LIMIT
        ),
    )(live, activations[0], cotangent[0], local_params[0], anchor.reshape(LIN, 128), momentum.reshape(LIN, 128))
    return new_params, new_anchor.reshape(1, 10, COLS), new_momentum.reshape(1, 10, COLS)


def solution(mesh):
    in_specs = (
        P("group", "fsdp", None),
        P("group", "fsdp", None),
        P("group", "fsdp"),
        P("group", "fsdp", None),
        P("fsdp", "group", None),
        P("fsdp", "group", None),
    )
    out_specs = (P("fsdp", None), P("fsdp", "group", None), P("fsdp", "group", None))
    return jax.shard_map(local, mesh=mesh, in_specs=in_specs, out_specs=out_specs, check_vma=False)
```

```python
import jax
import jax.numpy as jnp
from jax import lax
from jax.experimental import pallas as pl
from jax.experimental.pallas import tpu as pltpu
from jax.sharding import PartitionSpec as P

MESH = pl.DeviceIdType.MESH
BF, F32 = jnp.bfloat16, jnp.float32
SIZE = {"x": 4, "y": 8, "z": 8, "p": 8, "q": 8}
PARTS = (("xqp", (0,)), ("xpq", (1,)), ("pxq", (2,)), ("qxp", (3,)), ("pxq", (4,)))
LAST = (("p", (0, 3)), ("q", (1, 2, 4)))
UNITS = tuple(u for _, parts in LAST for p in parts for u in PARTS[p][1])
NU = len(UNITS)
HALVES = 1
PLAN = ("m0", "f00", "f10", "x", "m1", "n00", "n10", "m2", "m3", "t", "o",
        "f30", "n30", "f20", "n20", "f40", "n40", "q0", "f31", "n31", "f21", "n21", "f41", "n41", "f01", "q1",
        "f32", "n32", "f22", "n22", "f42", "n42", "f11", "s0", "q2", "f33", "f23", "f43", "q3",
        "s1", "s2", "s3", "s4", "c", "h0", "h1", "w", "b", "d", "e")


def tile(units):
    return (16 * len(units), 128)


TOK, ROWS, COLS, LIN = 160, 160, 1024, 80
VMEM_LIMIT = 56_000_000


def coords():
    g, f = lax.axis_index("group"), lax.axis_index("fsdp")
    return with_pq({"x": (f // 2) % 4, "y": g // 2, "z": (f // 8) * 2 + g % 2, "c": f % 2})


def with_pq(at):
    c, y, z = at["c"], at["y"], at["z"]
    return {**at, "p": z + c * (y - z), "q": y + c * (z - y)}


def device(at):
    return (at["y"] * 2 + at["z"] % 2, (at["z"] // 2) * 8 + at["x"] * 2 + at["c"])


def peer(here, axis, step):
    n, c = SIZE[axis], here["c"]
    if axis in "pq":
        dy = step * (c if axis == "p" else 1 - c)
        return device({**here, "y": (here["y"] + dy + 8) % 8, "z": (here["z"] + step - dy + 8) % 8})
    return device({**here, axis: (here[axis] + step + n) % n})


def loop(n, body, start=0):
    def step(i, carry):
        body(i)
        return carry

    lax.fori_loop(start, n, step, 0)


def put(src, dst, ssem, rsem, to):
    return pltpu.make_async_remote_copy(
        src_ref=src, dst_ref=dst, send_sem=ssem, recv_sem=rsem, device_id=to, device_id_type=MESH
    )


class Ring:
    def __init__(self, here, sign, axis, part, far, near, fs, fr, ns, nr):
        self.here, self.sign, self.axis, self.part = here, sign, axis, part
        self.n, self.me = SIZE[axis], here[axis]
        self.far, self.near = far, near
        self.sems = (fs, fr, ns, nr)
        self.width = part.shape[1] // HALVES

    def _cut(self, h):
        return slice(h * self.width, (h + 1) * self.width)

    def _far(self, k, h):
        t = (self.me + self.sign * (self.n // 2 - k) + self.n) % self.n
        to = peer(self.here, self.axis, self.sign)
        src, dst = self.part.at[t, self._cut(h)], self.far.at[k, self._cut(h)]
        return t, put(src, dst, self.sems[0].at[k, h], self.sems[1].at[k, h], to)

    def _near(self, k, h):
        t = (self.me - self.sign * (self.n // 2 - 1 - k) + self.n) % self.n
        to = peer(self.here, self.axis, -self.sign)
        src, dst = self.part.at[t, self._cut(h)], self.near.at[k, self._cut(h)]
        return t, put(src, dst, self.sems[2].at[k, h], self.sems[3].at[k, h], to)

    def _send(self, make, slots, k):
        copies = [make(k, h) for h in range(HALVES)]
        t = copies[0][0]
        if k:
            for h in range(HALVES):
                make(k - 1, h)[1].wait_recv()
            self.part[t] = self.part[t] + slots[k - 1]
        for _, copy in copies:
            copy.start()

    def send_far(self, k):
        self._send(self._far, self.far, k)

    def send_near(self, k):
        self._send(self._near, self.near, k)

    def finish(self):
        n = self.n // 2
        a, b = self.far.at[n - 1], self.near.at[n - 2]

        def body(i):
            total = self.part[self.me, i].astype(F32) + a[i].astype(F32) + b[i].astype(F32)
            self.part[self.me, i] = total.astype(BF)

        for h in range(HALVES):
            self._near(n - 2, h)[1].wait_recv()
            self._far(n - 1, h)[1].wait_recv()
        loop(self.part.shape[1], body)
        return self.part.at[self.me]

    def drain(self):
        for h in range(HALVES):
            for k in range(self.n // 2):
                self._far(k, h)[1].wait_send()
            for k in range(self.n // 2 - 1):
                self._near(k, h)[1].wait_send()


class Direct:
    def __init__(self, here, axis, part, slots, ss, rs):
        self.here, self.axis, self.part, self.slots = here, axis, part, slots
        self.n, self.me, self.ss, self.rs = SIZE[axis], here[axis], ss, rs

    def _copy(self, d):
        t = (self.me + d) % self.n
        to = peer(self.here, self.axis, d)
        return put(self.part.at[t], self.slots.at[d - 1], self.ss.at[d - 1], self.rs.at[d - 1], to)

    def start(self):
        loop(self.n, lambda d: self._copy(d).start(), 1)

    def arrive(self):
        loop(self.n, lambda d: self._copy(d).wait_recv(), 1)

    def total(self, i=None):
        at = (self.me,) if i is None else (self.me, i)
        acc = self.part[at].astype(F32)
        for d in range(self.n - 1):
            acc += self.slots[(d,) + at[1:]].astype(F32)
        return acc

    def drain(self):
        loop(self.n, lambda d: self._copy(d).wait_send(), 1)


def scratch():
    s = {}
    dma = pltpu.SemaphoreType.DMA
    s["a"], s["m"], s["lp"] = (pltpu.VMEM(v, BF) for v in ((TOK, 5120), (TOK, COLS), (ROWS, COLS)))
    s["anc"], s["mom"] = pltpu.VMEM((LIN, 128), F32), pltpu.VMEM((LIN, 128), F32)
    s["insem"] = dma((6,))
    s["at"] = pltpu.VMEM((2, 4, 4 * ROWS, TOK), BF)
    s["atp"] = pltpu.VMEM((4, 4 * ROWS, TOK), BF)
    s["live"] = pltpu.VMEM((1, 1), jnp.int32)
    s["mp"] = pltpu.VMEM((TOK, COLS), BF)
    s["exs"], s["exr"] = dma((6,)), dma((6,))
    s["cv"] = pltpu.VMEM((4, 8, 128), F32)
    s["cc"], s["cx"] = pltpu.VMEM((8, 128), F32), pltpu.VMEM((3, 8, 128), F32)
    s["cz"], s["cy"] = pltpu.VMEM((7, 8, 128), F32), pltpu.VMEM((7, 8, 128), F32)
    for k, n in (("cx", 3), ("cz", 7), ("cy", 7)):
        s[k + "s"], s[k + "r"] = dma((n,)), dma((n,))
    for p, (order, units) in enumerate(PARTS):
        n1, n2, n3 = (SIZE[k] for k in order)
        s[f"u{p}"] = pltpu.VMEM((n1, n2, n3) + tile(units), BF)
        s[f"far{p}"] = pltpu.VMEM((n1 // 2, n2, n3) + tile(units), BF)
        s[f"near{p}"] = pltpu.VMEM((n1 // 2 - 1, n2, n3) + tile(units), BF)
        s[f"fs{p}"], s[f"fr{p}"] = dma((n1 // 2, HALVES)), dma((n1 // 2, HALVES))
        s[f"ns{p}"], s[f"nr{p}"] = dma((n1 // 2 - 1, HALVES)), dma((n1 // 2 - 1, HALVES))
        s[f"two{p}"] = pltpu.VMEM((n2 - 1, n3) + tile(units), BF)
        s[f"ts{p}"], s[f"tr{p}"] = dma((n2 - 1,)), dma((n2 - 1,))
    for k, (_, parts) in enumerate(LAST):
        units = sum((PARTS[p][1] for p in parts), ())
        s[f"v{k}"] = pltpu.VMEM((8,) + tile(units), BF)
        s[f"three{k}"] = pltpu.VMEM((7,) + tile(units), BF)
        s[f"hs{k}"], s[f"hr{k}"] = dma((7,)), dma((7,))
    s["base"] = pltpu.VMEM((16, LIN, 128), BF)
    s["basef"] = pltpu.VMEM((ROWS * 8, 128), F32)
    s["bs"], s["br"] = dma((8,)), dma((8,))
    s["ag"] = pltpu.VMEM((16,) + tile(UNITS), BF)
    s["as"], s["ar"] = dma((15,)), dma((15,))
    s["avg"] = pltpu.VMEM((ROWS * 8, 128), F32)
    return s


NAMES = tuple(scratch())


def kernel(live_hbm, a_hbm, m_hbm, lp_hbm, anc_hbm, mom_hbm, np_ref, na_ref, nm_ref, *refs):
    s = dict(zip(NAMES, refs))
    anc_ref, mom_ref = s["anc"], s["mom"]
    here = coords()
    x, y, z, c = (here[k] for k in "xyzc")
    zl, g = z % 2, y * 2 + z % 2
    sign = 1 - 2 * c
    partner = device({**here, "c": 1 - c})

    def group_peer(j):
        other = (g + j) % 16
        return (other, lax.axis_index("fsdp"))

    bar = pltpu.get_barrier_semaphore()

    def greet(to):
        pl.semaphore_signal(bar, inc=1, device_id=to, device_id_type=MESH)

    greet(partner)
    loop(4, lambda d: greet(peer(here, "x", d)), 1)
    loop(8, lambda d: greet(peer(here, "z", d)), 1)
    loop(16, lambda j: greet(group_peer(j)), 1)

    wanted = ((live_hbm, s["live"]), (m_hbm, s["m"]), (a_hbm, s["a"]),
              (lp_hbm, s["lp"]), (anc_hbm, anc_ref), (mom_hbm, mom_ref))
    loads = [pltpu.make_async_copy(src, dst, s["insem"].at[i]) for i, (src, dst) in enumerate(wanted)]
    for load in loads:
        load.start()

    loads[0].wait()
    live = s["live"][...]
    s["cv"][0] = jnp.broadcast_to(live.astype(F32), (8, 128))
    loads[1].wait()
    row = lax.broadcasted_iota(jnp.int32, (TOK, COLS), 0)
    s["m"][...] = jnp.where(row < live, s["m"][...].astype(F32), 0.0).astype(BF)
    loads[2].wait()

    def transpose(k):
        t = s["a"][:, pl.ds(pl.multiple_of(k * 640, 128), 640)].T
        for j in range(4):
            at = pl.multiple_of((k % 2) * 320 + (j // 2) * 160, 16)
            s["at"][j % 2, k // 2, pl.ds(at, 160)] = t[j * 160:(j + 1) * 160]

    loop(8, transpose)
    for load in loads[3:]:
        load.wait()
    s["base"][g] = (-0.33 * anc_ref[...] - 0.567 * mom_ref[...]).astype(BF)

    pl.semaphore_wait(bar, 1 + 3 + 7 + 15)

    def rows_of(bx):
        return pl.ds(pl.multiple_of(bx * ROWS, 16), ROWS)

    def ex_copy(i, bx):
        rows = rows_of(bx)
        return put(s["at"].at[1 - c, :, rows], s["atp"].at[:, rows], s["exs"].at[2 + i], s["exr"].at[2 + i], partner)

    ex = [put(s["cv"].at[0], s["cc"], s["exs"].at[0], s["exr"].at[0], partner),
          put(s["m"], s["mp"], s["exs"].at[1], s["exr"].at[1], partner)]
    ex += [ex_copy(i, (x + dx + 4) % 4) for i, dx in enumerate((2, sign, -sign, 0))]
    for copy in ex[:4]:
        copy.start()

    zpartner = device({**here, "z": z + 1 - 2 * zl})
    base_z = put(s["base"].at[g], s["base"].at[g], s["bs"].at[7], s["br"].at[7], zpartner)

    def base_ring(k, way):
        pair = s["base"].at[pl.ds(2 * ((y - way * sign * k + 8) % 8), 2)]
        i = k if way > 0 else 4 + k
        return put(pair, pair, s["bs"].at[i], s["br"].at[i], peer(here, "y", way * sign))

    def base_step(k):
        if k == 0:
            base_z.wait_recv()
        else:
            base_ring(k - 1, 1).wait_recv()
            base_ring(k - 1, -1).wait_recv()
        base_ring(k, 1).start()
        if k < 3:
            base_ring(k, -1).start()

    def count_copy(key, axis, d, k):
        return put(s["cv"].at[k], s[key].at[d - 1], s[key + "s"].at[d - 1], s[key + "r"].at[d - 1], peer(here, axis, d))

    ex[0].wait_recv()
    s["cv"][1] = s["cv"][0] + s["cc"][...]
    loop(4, lambda d: count_copy("cx", "x", d, 1).start(), 1)
    base_z.start()

    rings = []
    for p, (order, _) in enumerate(PARTS):
        rings.append(Ring(here, sign, order[0], s[f"u{p}"], s[f"far{p}"], s[f"near{p}"],
                          s[f"fs{p}"], s[f"fr{p}"], s[f"ns{p}"], s[f"nr{p}"]))


    def store(out, bz, bx, r0, t0, width):
        for p, (order, units) in enumerate(PARTS):
            for i, u in enumerate(units):
                for q in range(2):
                    r = r0 + u * 32 + q * 16
                    for t in range(width):
                        at = with_pq({"x": bx, "y": t0 + t, "z": bz * 2 + q, "c": c})
                        s[f"u{p}"][at[order[0]], at[order[1]], at[order[2]], i * 16:i * 16 + 16] = (
                            out[r:r + 16, t * 128:(t + 1) * 128])

    def multiply(i):
        bx = (x + (2, -sign, sign, 0)[i] + 4) % 4
        rows = rows_of(bx)
        if i == 0:
            ex[1].wait_recv()
        ex_copy(i, bx).wait_recv()
        if i < 2:
            ex[4 + i].start()
        mine = s["at"][c, :, rows, :].reshape(4 * ROWS, TOK)
        theirs = s["atp"][:, rows, :].reshape(4 * ROWS, TOK)
        for h in range(4):
            cols = slice(h * 256, (h + 1) * 256)
            acc = jnp.dot(mine, s["m"][:, cols], preferred_element_type=F32)
            acc += jnp.dot(theirs, s["mp"][:, cols], preferred_element_type=F32)
            out = acc.astype(BF)
            for bz in range(4):
                store(out, bz, bx, bz * ROWS, h * 2, 2)

    def multiply_own(weight):
        rows = rows_of(x)
        for h in range(4):
            cols = slice(h * 256, (h + 1) * 256)
            acc = jnp.dot(s["at"][c, z // 2, rows], s["m"][:, cols], preferred_element_type=F32)
            acc += jnp.dot(s["atp"][z // 2, rows], s["mp"][:, cols], preferred_element_type=F32)
            acc -= weight * s["lp"][:, cols].astype(F32)
            store(acc.astype(BF), z // 2, x, 0, h * 2, 2)

    def far(u, k):
        rings[u].send_far(k)

    def near(u, k):
        rings[u].send_near(k)

    def second(p):
        part = rings[p].finish()
        twos[p] = Direct(here, PARTS[p][0][1], part, s[f"two{p}"], s[f"ts{p}"], s[f"tr{p}"])
        twos[p].start()

    def last(k):
        axis, parts = LAST[k]
        r = 0
        for p in parts:
            twos[p].arrive()
            rows = 16 * len(PARTS[p][1])

            def body(i, p=p, cut=slice(r, r + rows)):
                s[f"v{k}"][i, cut] = twos[p].total(i).astype(BF)

            loop(8, body)
            r += rows
        threes[k] = Direct(here, axis, s[f"v{k}"], s[f"three{k}"], s[f"hs{k}"], s[f"hr{k}"])
        threes[k].start()

    def ag_copy(j):
        mine = s["ag"].at[g]
        return put(mine, mine, s["as"].at[j - 1], s["ar"].at[j - 1], group_peer(j))

    def ag_in(j):
        theirs = s["ag"].at[(g - j + 16) % 16]
        return put(theirs, theirs, s["as"].at[j - 1], s["ar"].at[j - 1], group_peer(j))

    def averages():
        r = 0
        for k in range(len(LAST)):
            threes[k].arrive()
            rows = s[f"v{k}"].shape[1]
            s["ag"][g, r:r + rows] = (known["scale"] * threes[k].total()).astype(BF)
            r += rows
        for j in (8, 7, 9, 6, 10, 5, 11, 4, 12, 3, 13, 2, 14, 1, 15):
            ag_copy(j).start()

    def new_rows():
        loop(16, lambda j: ag_in(j).wait_recv(), 1)
        for i, u in enumerate(UNITS):
            for yy in range(8):
                for q in range(2):
                    r0 = u * 32 + q * 16
                    avg = s["ag"][yy * 2 + q, i * 16:i * 16 + 16].astype(F32)
                    s["avg"][pl.ds(r0 * 8 + yy, 16, stride=8), :] = avg
                    base = s["basef"][pl.ds(r0 * 8 + yy, 16, stride=8), :]
                    np_ref[r0:r0 + 16, yy * 128:(yy + 1) * 128] = (base + 1.33 * avg).astype(BF)

    twos, threes, known = {}, {}, {}

    def counts_x():
        loop(4, lambda d: count_copy("cx", "x", d, 1).wait_recv(), 1)
        s["cv"][2] = s["cv"][1] + s["cx"][0] + s["cx"][1] + s["cx"][2]
        loop(8, lambda d: count_copy("cz", "z", d, 2).start(), 1)

    def counts():
        loop(8, lambda d: count_copy("cz", "z", d, 2).wait_recv(), 1)
        cz = s["cz"]
        known["count"] = s["cv"][2] + cz[1] + cz[3] + cz[5]
        s["cv"][3] = known["count"] + cz[0] + cz[2] + cz[4] + cz[6]
        loop(8, lambda d: count_copy("cy", "y", d, 3).start(), 1)

    def total_count():
        loop(8, lambda d: count_copy("cy", "y", d, 3).wait_recv(), 1)
        total = s["cv"][3]
        for k in range(7):
            total += s["cy"][k]
        known["scale"] = (-0.5 / total)[0:1, 0:1]

    def base_rows():
        base_ring(3, 1).wait_recv()

        def widen(j):
            s["basef"][pl.ds(pl.multiple_of(j * LIN, 8), LIN), :] = s["base"][j].astype(F32)

        loop(16, widen)

    def drain():
        for r in rings:
            r.drain()
        for d in [*twos.values(), *threes.values()]:
            d.drain()
        for copy in ex:
            copy.wait_send()
        for key, axis, k, n in (("cx", "x", 1, 4), ("cz", "z", 2, 8), ("cy", "y", 3, 8)):
            loop(n, lambda d, key=key, axis=axis, k=k: count_copy(key, axis, d, k).wait_send(), 1)
        base_z.wait_send()
        for k in range(4):
            base_ring(k, 1).wait_send()
        for k in range(3):
            base_ring(k, -1).wait_send()

    steps = {
        "m": multiply, "q": base_step,
        "x": counts_x, "t": counts, "c": total_count, "b": base_rows, "d": drain,
        "o": lambda: multiply_own(2.0 * known["count"][0:1, 0:1]),
        "f": far, "n": near, "s": second, "h": last, "w": averages, "e": new_rows,
    }
    for step in PLAN:
        steps[step[0]](*(int(v) for v in step[1:]))

    own = s["avg"][pl.ds(pl.multiple_of(g * LIN, 8), LIN), :]
    anc = anc_ref[...]
    delta = anc - own
    moment = 0.9 * mom_ref[...] + delta
    nm_ref[...] = moment
    na_ref[...] = anc - 0.7 * (delta + 0.9 * moment)
    loop(16, lambda j: ag_copy(j).wait_send(), 1)


def local(activations, cotangent, live, local_params, anchor, momentum):
    vmem = pl.BlockSpec(memory_space=pltpu.VMEM)
    hbm = pl.BlockSpec(memory_space=pltpu.HBM)
    new_params, new_anchor, new_momentum = pl.pallas_call(
        kernel,
        name="outer_step",
        out_shape=(
            jax.ShapeDtypeStruct((ROWS, COLS), BF),
            jax.ShapeDtypeStruct((LIN, 128), F32),
            jax.ShapeDtypeStruct((LIN, 128), F32),
        ),
        in_specs=[hbm] * 6,
        out_specs=(vmem, vmem, vmem),
        scratch_shapes=list(scratch().values()),
        compiler_params=pltpu.CompilerParams(
            collective_id=0, has_side_effects=True, vmem_limit_bytes=VMEM_LIMIT
        ),
    )(live, activations[0], cotangent[0], local_params[0], anchor.reshape(LIN, 128), momentum.reshape(LIN, 128))
    return new_params, new_anchor.reshape(1, 10, COLS), new_momentum.reshape(1, 10, COLS)


def solution(mesh):
    in_specs = (
        P("group", "fsdp", None),
        P("group", "fsdp", None),
        P("group", "fsdp"),
        P("group", "fsdp", None),
        P("fsdp", "group", None),
        P("fsdp", "group", None),
    )
    out_specs = (P("fsdp", None), P("fsdp", "group", None), P("fsdp", "group", None))
    return jax.shard_map(local, mesh=mesh, in_specs=in_specs, out_specs=out_specs, check_vma=False)
```

```python
import jax
import jax.numpy as jnp
from jax import lax
from jax.experimental import pallas as pl
from jax.experimental.pallas import tpu as pltpu
from jax.sharding import PartitionSpec as P

MESH = pl.DeviceIdType.MESH
BF, F32 = jnp.bfloat16, jnp.float32
SIZE = {"x": 4, "y": 8, "z": 8, "p": 8, "q": 8}
PARTS = (("xqp", (0,)), ("xpq", (1,)), ("pxq", (2,)), ("qxp", (3,)), ("pxq", (4,)))
LAST = (("p", (0, 3)), ("q", (1, 2, 4)))
UNITS = tuple(u for _, parts in LAST for p in parts for u in PARTS[p][1])
NU = len(UNITS)
HALVES = 1
PLAN = ("m0", "f00", "f10", "x", "m1", "n00", "n10", "m2", "m3", "t", "o",
        "f30", "n30", "f20", "n20", "f40", "n40", "q0", "f31", "n31", "f21", "n21", "f41", "n41", "f01", "q1",
        "f32", "n32", "f22", "n22", "f42", "n42", "f11", "s0", "q2", "f33", "f23", "f43", "q3",
        "s1", "s2", "s3", "s4", "c", "h0", "h1", "w", "b", "d", "e")


def tile(units):
    return (16 * len(units), 128)


TOK, ROWS, COLS, LIN = 160, 160, 1024, 80
VMEM_LIMIT = 56_000_000


def coords():
    g, f = lax.axis_index("group"), lax.axis_index("fsdp")
    return with_pq({"x": (f // 2) % 4, "y": g // 2, "z": (f // 8) * 2 + g % 2, "c": f % 2})


def with_pq(at):
    c, y, z = at["c"], at["y"], at["z"]
    return {**at, "p": z + c * (y - z), "q": y + c * (z - y)}


def device(at):
    return (at["y"] * 2 + at["z"] % 2, (at["z"] // 2) * 8 + at["x"] * 2 + at["c"])


def peer(here, axis, step):
    n, c = SIZE[axis], here["c"]
    if axis in "pq":
        dy = step * (c if axis == "p" else 1 - c)
        return device({**here, "y": (here["y"] + dy + 8) % 8, "z": (here["z"] + step - dy + 8) % 8})
    return device({**here, axis: (here[axis] + step + n) % n})


def loop(n, body, start=0):
    def step(i, carry):
        body(i)
        return carry

    lax.fori_loop(start, n, step, 0)


def put(src, dst, ssem, rsem, to):
    return pltpu.make_async_remote_copy(
        src_ref=src, dst_ref=dst, send_sem=ssem, recv_sem=rsem, device_id=to, device_id_type=MESH
    )


class Ring:
    def __init__(self, here, sign, axis, part, far, near, fs, fr, ns, nr):
        self.here, self.sign, self.axis, self.part = here, sign, axis, part
        self.n, self.me = SIZE[axis], here[axis]
        self.far, self.near = far, near
        self.sems = (fs, fr, ns, nr)
        self.width = part.shape[1] // HALVES

    def _cut(self, h):
        return slice(h * self.width, (h + 1) * self.width)

    def _far(self, k, h):
        t = (self.me + self.sign * (self.n // 2 - k) + self.n) % self.n
        to = peer(self.here, self.axis, self.sign)
        src, dst = self.part.at[t, self._cut(h)], self.far.at[k, self._cut(h)]
        return t, put(src, dst, self.sems[0].at[k, h], self.sems[1].at[k, h], to)

    def _near(self, k, h):
        t = (self.me - self.sign * (self.n // 2 - 1 - k) + self.n) % self.n
        to = peer(self.here, self.axis, -self.sign)
        src, dst = self.part.at[t, self._cut(h)], self.near.at[k, self._cut(h)]
        return t, put(src, dst, self.sems[2].at[k, h], self.sems[3].at[k, h], to)

    def _send(self, make, slots, k):
        copies = [make(k, h) for h in range(HALVES)]
        t = copies[0][0]
        if k:
            for h in range(HALVES):
                make(k - 1, h)[1].wait_recv()
            self.part[t] = self.part[t] + slots[k - 1]
        for _, copy in copies:
            copy.start()

    def send_far(self, k):
        self._send(self._far, self.far, k)

    def send_near(self, k):
        self._send(self._near, self.near, k)

    def finish(self):
        n = self.n // 2
        a, b = self.far.at[n - 1], self.near.at[n - 2]

        def body(i):
            total = self.part[self.me, i].astype(F32) + a[i].astype(F32) + b[i].astype(F32)
            self.part[self.me, i] = total.astype(BF)

        for h in range(HALVES):
            self._near(n - 2, h)[1].wait_recv()
            self._far(n - 1, h)[1].wait_recv()
        loop(self.part.shape[1], body)
        return self.part.at[self.me]

    def drain(self):
        for h in range(HALVES):
            for k in range(self.n // 2):
                self._far(k, h)[1].wait_send()
            for k in range(self.n // 2 - 1):
                self._near(k, h)[1].wait_send()


class Direct:
    def __init__(self, here, axis, part, slots, ss, rs):
        self.here, self.axis, self.part, self.slots = here, axis, part, slots
        self.n, self.me, self.ss, self.rs = SIZE[axis], here[axis], ss, rs

    def _copy(self, d):
        t = (self.me + d) % self.n
        to = peer(self.here, self.axis, d)
        return put(self.part.at[t], self.slots.at[d - 1], self.ss.at[d - 1], self.rs.at[d - 1], to)

    def start(self):
        loop(self.n, lambda d: self._copy(d).start(), 1)

    def arrive(self):
        loop(self.n, lambda d: self._copy(d).wait_recv(), 1)

    def total(self, i=None):
        at = (self.me,) if i is None else (self.me, i)
        acc = self.part[at].astype(F32)
        for d in range(self.n - 1):
            acc += self.slots[(d,) + at[1:]].astype(F32)
        return acc

    def drain(self):
        loop(self.n, lambda d: self._copy(d).wait_send(), 1)


def scratch():
    s = {}
    dma = pltpu.SemaphoreType.DMA
    s["a"], s["m"], s["lp"] = (pltpu.VMEM(v, BF) for v in ((TOK, 5120), (TOK, COLS), (ROWS, COLS)))
    s["anc"], s["mom"] = pltpu.VMEM((LIN, 128), F32), pltpu.VMEM((LIN, 128), F32)
    s["insem"] = dma((6,))
    s["at"] = pltpu.VMEM((2, 4, 4 * ROWS, TOK), BF)
    s["atp"] = pltpu.VMEM((4, 4 * ROWS, TOK), BF)
    s["live"] = pltpu.VMEM((1, 1), jnp.int32)
    s["mp"] = pltpu.VMEM((TOK, COLS), BF)
    s["exs"], s["exr"] = dma((6,)), dma((6,))
    s["cv"] = pltpu.VMEM((4, 8, 128), F32)
    s["cc"], s["cx"] = pltpu.VMEM((8, 128), F32), pltpu.VMEM((3, 8, 128), F32)
    s["cz"], s["cy"] = pltpu.VMEM((7, 8, 128), F32), pltpu.VMEM((7, 8, 128), F32)
    for k, n in (("cx", 3), ("cz", 7), ("cy", 7)):
        s[k + "s"], s[k + "r"] = dma((n,)), dma((n,))
    for p, (order, units) in enumerate(PARTS):
        n1, n2, n3 = (SIZE[k] for k in order)
        s[f"u{p}"] = pltpu.VMEM((n1, n2, n3) + tile(units), BF)
        s[f"far{p}"] = pltpu.VMEM((n1 // 2, n2, n3) + tile(units), BF)
        s[f"near{p}"] = pltpu.VMEM((n1 // 2 - 1, n2, n3) + tile(units), BF)
        s[f"fs{p}"], s[f"fr{p}"] = dma((n1 // 2, HALVES)), dma((n1 // 2, HALVES))
        s[f"ns{p}"], s[f"nr{p}"] = dma((n1 // 2 - 1, HALVES)), dma((n1 // 2 - 1, HALVES))
        s[f"two{p}"] = pltpu.VMEM((n2 - 1, n3) + tile(units), BF)
        s[f"ts{p}"], s[f"tr{p}"] = dma((n2 - 1,)), dma((n2 - 1,))
    for k, (_, parts) in enumerate(LAST):
        units = sum((PARTS[p][1] for p in parts), ())
        s[f"v{k}"] = pltpu.VMEM((8,) + tile(units), BF)
        s[f"three{k}"] = pltpu.VMEM((7,) + tile(units), BF)
        s[f"hs{k}"], s[f"hr{k}"] = dma((7,)), dma((7,))
    s["base"] = pltpu.VMEM((16, LIN, 128), BF)
    s["basef"] = pltpu.VMEM((ROWS * 8, 128), F32)
    s["bs"], s["br"] = dma((8,)), dma((8,))
    s["ag"] = pltpu.VMEM((16,) + tile(UNITS), BF)
    s["as"], s["ar"] = dma((15,)), dma((15,))
    s["avg"] = pltpu.VMEM((ROWS * 8, 128), F32)
    return s


NAMES = tuple(scratch())


def kernel(live_hbm, a_hbm, m_hbm, lp_hbm, anc_hbm, mom_hbm, np_ref, na_ref, nm_ref, *refs):
    s = dict(zip(NAMES, refs))
    anc_ref, mom_ref = s["anc"], s["mom"]
    here = coords()
    x, y, z, c = (here[k] for k in "xyzc")
    zl, g = z % 2, y * 2 + z % 2
    sign = 1 - 2 * c
    partner = device({**here, "c": 1 - c})

    def group_peer(j):
        other = (g + j) % 16
        return (other, lax.axis_index("fsdp"))

    bar = pltpu.get_barrier_semaphore()

    def greet(to):
        pl.semaphore_signal(bar, inc=1, device_id=to, device_id_type=MESH)

    greet(partner)
    loop(4, lambda d: greet(peer(here, "x", d)), 1)
    loop(8, lambda d: greet(peer(here, "z", d)), 1)
    loop(16, lambda j: greet(group_peer(j)), 1)

    wanted = ((live_hbm, s["live"]), (m_hbm, s["m"]), (a_hbm, s["a"]),
              (lp_hbm, s["lp"]), (anc_hbm, anc_ref), (mom_hbm, mom_ref))
    loads = [pltpu.make_async_copy(src, dst, s["insem"].at[i]) for i, (src, dst) in enumerate(wanted)]
    for load in loads:
        load.start()

    loads[0].wait()
    live = s["live"][...]
    s["cv"][0] = jnp.broadcast_to(live.astype(F32), (8, 128))
    loads[1].wait()
    row = lax.broadcasted_iota(jnp.int32, (TOK, COLS), 0)
    s["m"][...] = jnp.where(row < live, s["m"][...].astype(F32), 0.0).astype(BF)
    loads[2].wait()

    def transpose(k):
        t = s["a"][:, pl.ds(pl.multiple_of(k * 640, 128), 640)].T
        for j in range(4):
            at = pl.multiple_of((k % 2) * 320 + (j // 2) * 160, 16)
            s["at"][j % 2, k // 2, pl.ds(at, 160)] = t[j * 160:(j + 1) * 160]

    loop(8, transpose)
    for load in loads[3:]:
        load.wait()
    s["base"][g] = (-0.33 * anc_ref[...] - 0.567 * mom_ref[...]).astype(BF)

    pl.semaphore_wait(bar, 1 + 3 + 7 + 15)

    def rows_of(bx):
        return pl.ds(pl.multiple_of(bx * ROWS, 16), ROWS)

    def ex_copy(i, bx):
        rows = rows_of(bx)
        return put(s["at"].at[1 - c, :, rows], s["atp"].at[:, rows], s["exs"].at[2 + i], s["exr"].at[2 + i], partner)

    ex = [put(s["cv"].at[0], s["cc"], s["exs"].at[0], s["exr"].at[0], partner),
          put(s["m"], s["mp"], s["exs"].at[1], s["exr"].at[1], partner)]
    ex += [ex_copy(i, (x + dx + 4) % 4) for i, dx in enumerate((2, sign, -sign, 0))]
    for copy in ex:
        copy.start()

    zpartner = device({**here, "z": z + 1 - 2 * zl})
    base_z = put(s["base"].at[g], s["base"].at[g], s["bs"].at[7], s["br"].at[7], zpartner)

    def base_ring(k, way):
        pair = s["base"].at[pl.ds(2 * ((y - way * sign * k + 8) % 8), 2)]
        i = k if way > 0 else 4 + k
        return put(pair, pair, s["bs"].at[i], s["br"].at[i], peer(here, "y", way * sign))

    def base_step(k):
        if k == 0:
            base_z.wait_recv()
        else:
            base_ring(k - 1, 1).wait_recv()
            base_ring(k - 1, -1).wait_recv()
        base_ring(k, 1).start()
        if k < 3:
            base_ring(k, -1).start()

    def count_copy(key, axis, d, k):
        return put(s["cv"].at[k], s[key].at[d - 1], s[key + "s"].at[d - 1], s[key + "r"].at[d - 1], peer(here, axis, d))

    ex[0].wait_recv()
    s["cv"][1] = s["cv"][0] + s["cc"][...]
    loop(4, lambda d: count_copy("cx", "x", d, 1).start(), 1)
    base_z.start()

    rings = []
    for p, (order, _) in enumerate(PARTS):
        rings.append(Ring(here, sign, order[0], s[f"u{p}"], s[f"far{p}"], s[f"near{p}"],
                          s[f"fs{p}"], s[f"fr{p}"], s[f"ns{p}"], s[f"nr{p}"]))


    def store(out, bz, bx, r0, t0, width):
        for p, (order, units) in enumerate(PARTS):
            for i, u in enumerate(units):
                for q in range(2):
                    r = r0 + u * 32 + q * 16
                    for t in range(width):
                        at = with_pq({"x": bx, "y": t0 + t, "z": bz * 2 + q, "c": c})
                        s[f"u{p}"][at[order[0]], at[order[1]], at[order[2]], i * 16:i * 16 + 16] = (
                            out[r:r + 16, t * 128:(t + 1) * 128])

    def multiply(i):
        bx = (x + (2, -sign, sign, 0)[i] + 4) % 4
        rows = rows_of(bx)
        if i == 0:
            ex[1].wait_recv()
        ex_copy(i, bx).wait_recv()
        mine = s["at"][c, :, rows, :].reshape(4 * ROWS, TOK)
        theirs = s["atp"][:, rows, :].reshape(4 * ROWS, TOK)
        for h in range(4):
            cols = slice(h * 256, (h + 1) * 256)
            acc = jnp.dot(mine, s["m"][:, cols], preferred_element_type=F32)
            acc += jnp.dot(theirs, s["mp"][:, cols], preferred_element_type=F32)
            out = acc.astype(BF)
            for bz in range(4):
                store(out, bz, bx, bz * ROWS, h * 2, 2)

    def multiply_own(weight):
        rows = rows_of(x)
        for h in range(4):
            cols = slice(h * 256, (h + 1) * 256)
            acc = jnp.dot(s["at"][c, z // 2, rows], s["m"][:, cols], preferred_element_type=F32)
            acc += jnp.dot(s["atp"][z // 2, rows], s["mp"][:, cols], preferred_element_type=F32)
            acc -= weight * s["lp"][:, cols].astype(F32)
            store(acc.astype(BF), z // 2, x, 0, h * 2, 2)

    def far(u, k):
        rings[u].send_far(k)

    def near(u, k):
        rings[u].send_near(k)

    def second(p):
        part = rings[p].finish()
        twos[p] = Direct(here, PARTS[p][0][1], part, s[f"two{p}"], s[f"ts{p}"], s[f"tr{p}"])
        twos[p].start()

    def last(k):
        axis, parts = LAST[k]
        r = 0
        for p in parts:
            twos[p].arrive()
            rows = 16 * len(PARTS[p][1])

            def body(i, p=p, cut=slice(r, r + rows)):
                s[f"v{k}"][i, cut] = twos[p].total(i).astype(BF)

            loop(8, body)
            r += rows
        threes[k] = Direct(here, axis, s[f"v{k}"], s[f"three{k}"], s[f"hs{k}"], s[f"hr{k}"])
        threes[k].start()

    def ag_copy(j):
        mine = s["ag"].at[g]
        return put(mine, mine, s["as"].at[j - 1], s["ar"].at[j - 1], group_peer(j))

    def ag_in(j):
        theirs = s["ag"].at[(g - j + 16) % 16]
        return put(theirs, theirs, s["as"].at[j - 1], s["ar"].at[j - 1], group_peer(j))

    def averages():
        r = 0
        for k in range(len(LAST)):
            threes[k].arrive()
            rows = s[f"v{k}"].shape[1]
            s["ag"][g, r:r + rows] = (known["scale"] * threes[k].total()).astype(BF)
            r += rows
        for j in (8, 7, 9, 6, 10, 5, 11, 4, 12, 3, 13, 2, 14, 1, 15):
            ag_copy(j).start()

    def new_rows():
        loop(16, lambda j: ag_in(j).wait_recv(), 1)
        for i, u in enumerate(UNITS):
            for yy in range(8):
                for q in range(2):
                    r0 = u * 32 + q * 16
                    avg = s["ag"][yy * 2 + q, i * 16:i * 16 + 16].astype(F32)
                    s["avg"][pl.ds(r0 * 8 + yy, 16, stride=8), :] = avg
                    base = s["basef"][pl.ds(r0 * 8 + yy, 16, stride=8), :]
                    np_ref[r0:r0 + 16, yy * 128:(yy + 1) * 128] = (base + 1.33 * avg).astype(BF)

    twos, threes, known = {}, {}, {}

    def counts_x():
        loop(4, lambda d: count_copy("cx", "x", d, 1).wait_recv(), 1)
        s["cv"][2] = s["cv"][1] + s["cx"][0] + s["cx"][1] + s["cx"][2]
        loop(8, lambda d: count_copy("cz", "z", d, 2).start(), 1)

    def counts():
        loop(8, lambda d: count_copy("cz", "z", d, 2).wait_recv(), 1)
        cz = s["cz"]
        known["count"] = s["cv"][2] + cz[1] + cz[3] + cz[5]
        s["cv"][3] = known["count"] + cz[0] + cz[2] + cz[4] + cz[6]
        loop(8, lambda d: count_copy("cy", "y", d, 3).start(), 1)

    def total_count():
        loop(8, lambda d: count_copy("cy", "y", d, 3).wait_recv(), 1)
        total = s["cv"][3]
        for k in range(7):
            total += s["cy"][k]
        known["scale"] = (-0.5 / total)[0:1, 0:1]

    def base_rows():
        base_ring(3, 1).wait_recv()

        def widen(j):
            s["basef"][pl.ds(pl.multiple_of(j * LIN, 8), LIN), :] = s["base"][j].astype(F32)

        loop(16, widen)

    def drain():
        for r in rings:
            r.drain()
        for d in [*twos.values(), *threes.values()]:
            d.drain()
        for copy in ex:
            copy.wait_send()
        for key, axis, k, n in (("cx", "x", 1, 4), ("cz", "z", 2, 8), ("cy", "y", 3, 8)):
            loop(n, lambda d, key=key, axis=axis, k=k: count_copy(key, axis, d, k).wait_send(), 1)
        base_z.wait_send()
        for k in range(4):
            base_ring(k, 1).wait_send()
        for k in range(3):
            base_ring(k, -1).wait_send()

    steps = {
        "m": multiply, "q": base_step,
        "x": counts_x, "t": counts, "c": total_count, "b": base_rows, "d": drain,
        "o": lambda: multiply_own(2.0 * known["count"][0:1, 0:1]),
        "f": far, "n": near, "s": second, "h": last, "w": averages, "e": new_rows,
    }
    for step in PLAN:
        steps[step[0]](*(int(v) for v in step[1:]))

    own = s["avg"][pl.ds(pl.multiple_of(g * LIN, 8), LIN), :]
    anc = anc_ref[...]
    delta = anc - own
    moment = 0.9 * mom_ref[...] + delta
    nm_ref[...] = moment
    na_ref[...] = anc - 0.7 * (delta + 0.9 * moment)
    loop(16, lambda j: ag_copy(j).wait_send(), 1)


def local(activations, cotangent, live, local_params, anchor, momentum):
    vmem = pl.BlockSpec(memory_space=pltpu.VMEM)
    hbm = pl.BlockSpec(memory_space=pltpu.HBM)
    new_params, new_anchor, new_momentum = pl.pallas_call(
        kernel,
        name="outer_step",
        out_shape=(
            jax.ShapeDtypeStruct((ROWS, COLS), BF),
            jax.ShapeDtypeStruct((LIN, 128), F32),
            jax.ShapeDtypeStruct((LIN, 128), F32),
        ),
        in_specs=[hbm] * 6,
        out_specs=(vmem, vmem, vmem),
        scratch_shapes=list(scratch().values()),
        compiler_params=pltpu.CompilerParams(
            collective_id=0, has_side_effects=True, vmem_limit_bytes=VMEM_LIMIT
        ),
    )(live, activations[0], cotangent[0], local_params[0], anchor.reshape(LIN, 128), momentum.reshape(LIN, 128))
    return new_params, new_anchor.reshape(1, 10, COLS), new_momentum.reshape(1, 10, COLS)


def solution(mesh):
    in_specs = (
        P("group", "fsdp", None),
        P("group", "fsdp", None),
        P("group", "fsdp"),
        P("group", "fsdp", None),
        P("fsdp", "group", None),
        P("fsdp", "group", None),
    )
    out_specs = (P("fsdp", None), P("fsdp", "group", None), P("fsdp", "group", None))
    return jax.shard_map(local, mesh=mesh, in_specs=in_specs, out_specs=out_specs, check_vma=False)
```
